256 devices in a mesh: dp: 16 (over x, z_hi, core), fsdp: 16 (over y, z_lo).
Axes of the slice: x: 4, y: 4, z: 8 (z_hi: 2, z_lo: 4; z = z_hi * 4 + z_lo), core: 2. Of those that a mesh axis runs over, the one named last changes fastest.
Arguments:
- query_key_value: bfloat16 [3, 114688, 1664], P(None, ('dp', 'fsdp')), may hold values from -60 to 60
- cotangent: bfloat16 [114688, 3200], P(('dp', 'fsdp')), may hold values from -24 to 24
- proj_weight: bfloat16 [1664, 3200], P('fsdp'), may hold values from -0.15625 to 0.15625
- layer_scale: float32 [3200], replicated, may hold values from 0.3 to 3
- lengths: int32 [16, 16, 4], P(None, 'fsdp'), may hold values from 0 to 192, as said below
Outputs:
- grad_qkv: bfloat16 [3, 114688, 1664], P(None, ('dp', 'fsdp'))
- grad_proj: float32 [1664, 3200], P('fsdp', 'dp')
The draws below stay inside these ranges and needn't reach their ends.
Inputs may be any that keep to these rules, and one draw needn't show every extreme that they name: lengths[a, b, 0] + lengths[a, b, 1] = 256, each at least 64; lengths[a, b, 2] and lengths[a, b, 3] are both 0 or both from 64 to 96; of the devices a and a + 16 / 2 (a < 8) of one fsdp index exactly one has them nonzero; in every fsdp index the nonzero one of the pair a = 0 has lengths[., b, 3] = 96.
All inputs are finite; a program needn't handle non-finite values.
Results may differ from the reference program's by a relative error of at most 0.011.
Values may be sent and summed in bfloat16 or wider, within the bound.
A program may use at most 128 MiB of HBM per device.

```python
import math
import jax
import jax.numpy as jnp
from jax import lax

D = 3200
HEADS = 13
HS = 128
HD = 1664
MAIN = 256
SLOT = 96
TOK_DEV = 448
TOKENS = 114688
N_DP = 16
N_FSDP = 16


def draw_lengths(key, part):
    key = jax.random.fold_in(key, 11)
    first_key, second_key, third_key = jax.random.split(key, 3)
    low = MAIN // 4
    first = jax.random.randint(first_key, (N_DP, N_FSDP, 1), low, MAIN - low + 1)
    second = MAIN - first
    tail_low = 2 * SLOT // 3
    tails = jax.random.randint(second_key, (N_DP, N_FSDP, 2), tail_low, SLOT + 1)
    half = N_DP // 2
    flips = jax.random.randint(third_key, (half, N_FSDP, 1), 0, 2)
    flips_full = jnp.concatenate([flips, flips], axis=0)
    rows = jnp.arange(N_DP)[:, None, None]
    heavy = jnp.where(rows < half, flips_full == 0, flips_full == 1)
    pinned = (rows % half == 0) & (jnp.arange(2)[None, None, :] == 1)
    tails = jnp.where(pinned, SLOT, tails)
    tails = jnp.where(heavy, tails, 0)
    return jnp.concatenate([first, second, tails], axis=2).astype(jnp.int32)


def draw_query_key_value(key, part):
    key = jax.random.fold_in(key, 5)
    first_key = jax.random.fold_in(key, 0)
    return jnp.clip(jax.random.normal(first_key, (3, TOKENS, HEADS * HS)), -6.0, 6.0).astype(jnp.bfloat16)


def with_spikes(values, stream_key, source, target, shards_of, factor):
    def block_of(position):
        return (jnp.arange(values.shape[position]) // (values.shape[position] // shards_of)).reshape((-1,) + (1,) * (values.ndim - 1 - position))

    first = jax.random.permutation(stream_key, shards_of)[block_of(target)]
    far = (block_of(target) + shards_of // 2) % shards_of
    return jnp.where((block_of(source) == first) | (block_of(source) == far), factor * values, values)


def level_of(stream_key, dims, cuts, low, top_value):
    def one(position, parts):
        heights = jax.random.uniform(jax.random.fold_in(jax.random.fold_in(stream_key, 6), position), (parts,), jnp.float32, low / len(cuts), top_value / len(cuts))
        return jnp.repeat(jnp.exp(heights), dims[position] // parts).reshape((-1,) + (1,) * (len(dims) - position - 1))

    level = one(*cuts[0])
    for cut in cuts[1:]:
        level = level * one(*cut)
    return level


def scatter_about(key, extent, width, reach, shards=(), kind=jnp.bfloat16):
    factor_of = level_of(key, extent, shards, -0.22, 0.18) if shards else 1.0
    result = jax.random.normal(key, extent, jnp.float32) * width * factor_of
    return jnp.minimum(jnp.maximum(result, -reach), reach).astype(kind)


def gaussian_with(rng, shape, scale, limit, cuts, heavy, held_as=jnp.bfloat16):
    values = scale * jax.random.normal(rng, shape, jnp.float32)
    if cuts:
        values = values * level_of(rng, shape, cuts, -0.22, 0.18)
    return jnp.clip(with_spikes(values, jax.random.fold_in(rng, 3), *heavy), -limit, limit).astype(held_as)


def setup_inputs(seed: int = 0) -> dict:
    splits = jax.random.split(jax.random.key(seed), 6)
    query_key_value = draw_query_key_value(jax.random.fold_in(splits[5], 71), 0)
    cotangent = gaussian_with(splits[1], (TOKENS, D), 1.0, 24.0, ((0, 256),), (0, 1, 128, 5.5))
    proj_weight = scatter_about(splits[2], (HD, D), HD ** -0.5, 0.15625, ((0, 16),))
    layer_scale = jnp.clip(jnp.exp(jax.random.uniform(splits[3], (D,), jnp.float32, math.log(0.3), math.log(3.0))), 0.3, 3.0)
    lengths = draw_lengths(jax.random.fold_in(splits[5], 71), 0)
    return {"query_key_value": query_key_value, "cotangent": cotangent, "proj_weight": proj_weight, "layer_scale": layer_scale, "lengths": lengths}


def segments(counts):
    main_pos = jnp.arange(MAIN, dtype=jnp.int32)
    slot_pos = jnp.arange(SLOT, dtype=jnp.int32)
    main_ids = (main_pos >= counts[0]).astype(jnp.int32)
    first_ids = jnp.where(slot_pos < counts[2], 2, -1).astype(jnp.int32)
    second_ids = jnp.where(slot_pos < counts[3], 3, -1).astype(jnp.int32)
    return jnp.concatenate([main_ids, first_ids, second_ids])


def attend(query_rows, key_rows, value_rows, grad_rows, segment):
    rows = query_rows.shape[0]
    factor = HS ** -0.5
    query_h = query_rows.reshape(rows, HEADS, HS).astype(jnp.float32)
    key_h = key_rows.reshape(rows, HEADS, HS).astype(jnp.float32)
    value_h = value_rows.reshape(rows, HEADS, HS).astype(jnp.float32)
    grad_h = grad_rows.reshape(rows, HEADS, HS).astype(jnp.float32)
    scores = jnp.einsum("qhd,khd->hqk", query_h, key_h) * factor
    valid = segment >= 0
    allowed = (segment[:, None] == segment[None, :]) & valid[:, None]
    scores = jnp.where(allowed[None], scores, -1e30)
    highest = jnp.max(scores, axis=2, keepdims=True)
    weights = jnp.exp(scores - highest)
    probs = weights / jnp.sum(weights, axis=2, keepdims=True)
    probs = jnp.where(valid[None, :, None], probs, jnp.zeros_like(probs))
    probs_b = probs.astype(jnp.bfloat16).astype(jnp.float32)
    attended = jnp.einsum("hqk,khd->qhd", probs_b, value_h).reshape(rows, HD).astype(jnp.bfloat16)
    dprob = jnp.einsum("qhd,khd->hqk", grad_h, value_h)
    delta = jnp.sum(probs * dprob, axis=2, keepdims=True)
    dscore = (probs * (dprob - delta) * factor).astype(jnp.bfloat16).astype(jnp.float32)
    grad_query = jnp.einsum("hqk,khd->qhd", dscore, key_h).reshape(rows, HD).astype(jnp.bfloat16)
    grad_key = jnp.einsum("hqk,qhd->khd", dscore, query_h).reshape(rows, HD).astype(jnp.bfloat16)
    grad_value = jnp.einsum("hqk,qhd->khd", probs_b, grad_h).reshape(rows, HD).astype(jnp.bfloat16)
    return attended, grad_query, grad_key, grad_value


def reference(query_key_value, cotangent, proj_weight, layer_scale, lengths):
    scaled = (cotangent.astype(jnp.float32) * layer_scale[None, :]).astype(jnp.bfloat16)
    grad_out = jnp.dot(scaled, proj_weight.T, preferred_element_type=jnp.float32).astype(jnp.bfloat16)
    groups_all = N_DP * N_FSDP
    split = query_key_value.reshape(3, groups_all, TOK_DEV, HD)
    grad_groups = grad_out.reshape(groups_all, TOK_DEV, HD)
    scaled_groups = scaled.reshape(groups_all, TOK_DEV, D)
    counts_all = lengths.reshape(groups_all, 4)

    def one_group(total, items):
        query_rows, key_rows, value_rows, grad_rows, scaled_rows, counts = items
        segment = segments(counts)
        attended, grad_query, grad_key, grad_value = attend(query_rows, key_rows, value_rows, grad_rows, segment)
        term = jnp.dot(attended.T, scaled_rows, preferred_element_type=jnp.float32)
        return total + term, jnp.stack([grad_query, grad_key, grad_value])

    total, stacked = lax.scan(one_group, jnp.zeros((HD, D), jnp.float32),
                              (split[0], split[1], split[2], grad_groups, scaled_groups, counts_all))
    grad_qkv = jnp.transpose(stacked, (1, 0, 2, 3)).reshape(3, TOKENS, HD)
    return grad_qkv, total
```

```python
import jax
import jax.numpy as jnp
from jax import lax
from jax.experimental import pallas as pl
from jax.experimental.pallas import tpu as pltpu
from jax.sharding import PartitionSpec as P

HS = 128
HEADS = 13
HD = HS * HEADS
D = 3200
MAIN = 256
SLOT = 96
TAIL = 2 * SLOT
ROWS = MAIN + TAIL
SHARD = HD // 16
HALF = 13 * 128
FIRST = 7 * 128
LAST = HALF - FIRST
WIN = 7 * 128
STEP = 6 * 128
CHUNK = 208
FACTOR = HS ** (-0.5)
MESH = pl.DeviceIdType.MESH
F32 = jnp.float32
BF16 = jnp.bfloat16

A1, B1, A2, A3, B2, B3 = 0, 3, 7, 9, 11, 13
COT, ATT, GRAD, XS, YS, ZS, FIN = 15, 16, 20, 21, 33, 36, 43
N_MSG = 44


def dot_nn(a, b):
    return lax.dot_general(a, b, (((1,), (0,)), ((), ())), preferred_element_type=F32)


def dot_nt(a, b):
    return lax.dot_general(a, b, (((1,), (1,)), ((), ())), preferred_element_type=F32)


def dot_tn(a, b):
    return lax.dot_general(a, b, (((0,), (0,)), ((), ())), preferred_element_type=F32)


def kernel(
    qkv_hbm, cot_hbm, w_hbm, scale_ref, lens_ref, grad_hbm, proj_ref,
    qkv, scaled, att, p_main, p_tail, w_a, w_b, w_all, go_own, go_out, go_in,
    x_own, x_in, y_own, y_in, z_own, z_in, total, send, recv, local,
):
    dp, member = lax.axis_index("dp"), lax.axis_index("fsdp")
    x, z_hi, core = dp // 4, (dp // 2) % 2, dp % 2
    y, z_lo = member // 4, member % 4
    z = z_hi * 4 + z_lo

    def at_x(k):
        return (lax.rem(x + k, 4) * 4 + z_hi * 2 + core, member)

    def at_y(k):
        return (dp, lax.rem(y + k, 4) * 4 + z_lo)

    def at_z(k):
        t = lax.rem(z + k, 8)
        return (x * 4 + (t // 4) * 2 + core, y * 4 + t % 4)

    sibling = (x * 4 + z_hi * 2 + 1 - core, member)

    def remote(src, dst, index, device):
        return pltpu.make_async_remote_copy(
            src_ref=src, dst_ref=dst, send_sem=send.at[index], recv_sem=recv.at[index],
            device_id=device, device_id_type=MESH,
        )

    def launch(*args):
        copy = remote(*args)
        copy.start()
        return copy

    load_qkv = pltpu.make_async_copy(qkv_hbm, qkv, local.at[0])
    load_qkv.start()
    load_cot = pltpu.make_async_copy(cot_hbm, scaled.at[0], local.at[1])
    load_cot.start()

    col = pl.multiple_of(core * (12 * 128), 128)
    part_a = w_hbm.at[:, pl.ds(col, FIRST)]
    part_b = w_hbm.at[:, pl.ds(col + FIRST, LAST)]
    load_a = pltpu.make_async_copy(part_a, w_a.at[z_lo, y], local.at[2])
    load_a.start()
    load_b = pltpu.make_async_copy(part_b, w_b.at[y, z_lo], local.at[3])
    load_b.start()

    peers = [sibling, at_x(1), at_x(3)] + [at_y(k) for k in (1, 2, 3)] + [at_z(k) for k in range(1, 8)]
    barrier = pltpu.get_barrier_semaphore()
    for peer in peers:
        pl.semaphore_signal(barrier, inc=1, device_id=peer, device_id_type=MESH)
    pl.semaphore_wait(barrier, len(peers))

    sent = []
    gather_a = [launch(part_a, w_a.at[z_lo, y], A1 + i, at_y(k)) for i, k in enumerate((1, 3, 2))]
    small = LAST // 2
    gather_b = [launch(part_b, w_b.at[y, z_lo], B1 + i, at_z(k)) for i, k in enumerate((1, 7))]
    for i, k in enumerate((2, 6)):
        piece = w_hbm.at[:, pl.ds(col + FIRST + i * small, small)]
        gather_b.append(launch(piece, w_b.at[y, z_lo, :, pl.ds(i * small, small)], B1 + 2 + i, at_z(k)))
    cot_copy = launch(cot_hbm, scaled.at[1], COT, sibling)
    sent += gather_a + gather_b + [cot_copy]

    first_count = lens_ref[dp, 0]
    count_2, count_3 = lens_ref[dp, 2], lens_ref[dp, 3]

    def main_mask():
        rows = lax.broadcasted_iota(jnp.int32, (MAIN, MAIN), 0)
        cols = lax.broadcasted_iota(jnp.int32, (MAIN, MAIN), 1)
        one = jnp.where(rows >= first_count, 1, 0)
        two = jnp.where(cols >= first_count, 1, 0)
        return one == two

    def tail_mask():
        def ids(axis):
            at = lax.broadcasted_iota(jnp.int32, (TAIL, TAIL), axis)
            first = jnp.where(at < count_2, 2, -1)
            second = jnp.where(at - SLOT < count_3, 3, -1)
            return jnp.where(at < SLOT, first, second)

        one, two = ids(0), ids(1)
        return (one == two) & (one >= 0)

    def soft(query, key, allowed):
        scores = jnp.where(allowed, dot_nt(query, key) * FACTOR, -1e30)
        highest = jnp.max(scores, axis=1, keepdims=True)
        weights = jnp.where(allowed, jnp.exp(scores - highest), 0.0)
        norm = jnp.sum(weights, axis=1, keepdims=True)
        return weights * (1.0 / jnp.where(norm > 0.0, norm, 1.0))

    load_qkv.wait()

    def forward(head, _):
        lanes = pl.ds(pl.multiple_of(head * HS, HS), HS)
        query, key, value = qkv[0, :, lanes], qkv[1, :, lanes], qkv[2, :, lanes]
        probs = soft(query[:MAIN], key[:MAIN], main_mask())
        probs_t = soft(query[MAIN:], key[MAIN:], tail_mask())
        p_main[head] = probs
        p_tail[head] = probs_t
        out = dot_nn(probs.astype(BF16), value[:MAIN])
        out_t = dot_nn(probs_t.astype(BF16), value[MAIN:])
        att[0, lanes, :] = jnp.concatenate([out, out_t], axis=0).T.astype(BF16)
        return 0

    lax.fori_loop(0, HEADS, forward, 0)

    att_copies = []
    for k in range(4):
        rows = pl.ds(pl.multiple_of(416 * k + CHUNK * (1 - core), 16), CHUNK)
        att_copies.append(launch(att.at[0, rows], att.at[1, rows], ATT + k, sibling))
    sent += att_copies

    def scale_rows(part):
        def one(step, _):
            rows = pl.ds(pl.multiple_of(step * 64, 64), 64)
            scaled[part, rows, :] = (scaled[part, rows, :].astype(F32) * scale_ref[...]).astype(BF16)
            return 0

        lax.fori_loop(0, ROWS // 64, one, 0)

    load_cot.wait()
    scale_rows(0)

    load_a.wait()
    load_b.wait()
    for copy in gather_a:
        copy.wait_recv()
    wide_a = [launch(w_a.at[z_lo], w_a.at[z_lo], A2 + i, at_z(k)) for i, k in enumerate((1, 7))]
    for copy in gather_b:
        copy.wait_recv()
    wide_b = [launch(w_b.at[y], w_b.at[y], B2 + i, at_y(k)) for i, k in enumerate((1, 3))]
    sent += wide_a + wide_b

    cot_copy.wait_recv()
    scale_rows(1)
    for copy in att_copies:
        copy.wait_recv()

    hops = []
    for i in range(4):
        block = lax.rem(y + 1 + i, 4)
        way = 1 if i % 2 == 0 else 3
        rows = pl.ds(pl.multiple_of(416 * block + CHUNK * core, 16), CHUNK)
        hop = []
        for j, k in enumerate((2, 4 - way, way, 0)):
            cols = pl.ds(pl.multiple_of(lax.rem(x + k, 4) * STEP, 128), WIN)
            term = dot_nn(att[0, rows, :], scaled[0, :, cols]) + dot_nn(att[1, rows, :], scaled[1, :, cols])
            x_own[i, j] = term.astype(BF16)
            if j < 2:
                hop.append(launch(x_own.at[i, j], x_in.at[i, j], XS + 3 * i + j, at_x(way if j == 0 else 4 - way)))
        hops.append(hop)

    def pass_on(i):
        way = 1 if i % 2 == 0 else 3
        hops[i][0].wait_recv()

        def add(step, _):
            rows = pl.ds(pl.multiple_of(step * 16, 16), 16)
            x_own[i, 2, rows, :] = (x_own[i, 2, rows, :].astype(F32) + x_in[i, 0, rows, :].astype(F32)).astype(BF16)
            return 0

        lax.fori_loop(0, CHUNK // 16, add, 0)
        hops[i].append(launch(x_own.at[i, 2], x_in.at[i, 2], XS + 3 * i + 2, at_x(way)))

    y_copies = []

    def finish_x(i):
        hops[i][1].wait_recv()
        hops[i][2].wait_recv()

        def add(step, _):
            rows = pl.ds(pl.multiple_of(step * 16, 16), 16)
            term = x_own[i, 3, rows, :].astype(F32) + x_in[i, 1, rows, :].astype(F32) + x_in[i, 2, rows, :].astype(F32)
            y_own[i, rows, :] = term.astype(BF16)
            return 0

        lax.fori_loop(0, CHUNK // 16, add, 0)
        if i < 3:
            y_copies.append(launch(y_own.at[i], y_in.at[i], YS + i, at_y(1 + i)))

    pass_on(0)

    wide_a[0].wait_recv()
    behind, ahead = lax.rem(z_lo + 3, 4), lax.rem(z_lo + 1, 4)
    far_a = [launch(w_a.at[behind, pl.ds(0, 2)], w_a.at[behind, pl.ds(0, 2)], A3, at_z(1))]
    wide_a[1].wait_recv()
    far_a.append(launch(w_a.at[ahead, pl.ds(2, 2)], w_a.at[ahead, pl.ds(2, 2)], A3 + 1, at_z(7)))
    behind, ahead = lax.rem(y + 3, 4), lax.rem(y + 1, 4)
    wide_b[0].wait_recv()
    far_b = [launch(w_b.at[behind, pl.ds(0, 2)], w_b.at[behind, pl.ds(0, 2)], B3, at_y(1))]
    wide_b[1].wait_recv()
    far_b.append(launch(w_b.at[ahead, pl.ds(2, 2)], w_b.at[ahead, pl.ds(2, 2)], B3 + 1, at_y(3)))
    sent += far_a + far_b

    pass_on(1)
    finish_x(0)
    for copy in far_a + far_b:
        copy.wait_recv()

    for block in range(4):
        rows = slice(416 * block, 416 * block + 416)
        left = jnp.concatenate([w_a[k, block].astype(F32) for k in range(4)], axis=0)
        w_all[rows, :FIRST] = left.astype(BF16)
        right = jnp.concatenate([w_b[block, k].astype(F32) for k in range(4)], axis=0)
        w_all[rows, FIRST:] = right.astype(BF16)

    keep = jnp.where(core == 1, 0.0, 1.0)
    w_all[:, :128] = (w_all[:, :128].astype(F32) * keep).astype(BF16)

    cols = pl.ds(col, HALF)
    cuts = ((0, 512), (512, 512), (1024, 640))
    for low, size in cuts:
        go_out[:, low:low + size] = dot_nt(scaled[1, :, cols], w_all[low:low + size, :]).astype(BF16)
    go_copy = launch(go_out, go_in, GRAD, sibling)
    sent.append(go_copy)
    for low, size in cuts:
        go_own[:, low:low + size] = dot_nt(scaled[0, :, cols], w_all[low:low + size, :])

    pass_on(2)
    finish_x(1)
    go_copy.wait_recv()

    def grads(query, key, value, grad, probs):
        dprob = dot_nt(grad, value)
        delta = jnp.sum(probs * dprob, axis=1, keepdims=True)
        dscore = (probs * (dprob - delta) * FACTOR).astype(BF16)
        return dot_nn(dscore, key), dot_tn(dscore, query), dot_tn(probs.astype(BF16), grad)

    def backward(head, _):
        lanes = pl.ds(pl.multiple_of(head * HS, HS), HS)
        query, key, value = qkv[0, :, lanes], qkv[1, :, lanes], qkv[2, :, lanes]
        grad = (go_own[:, lanes] + go_in[:, lanes].astype(F32)).astype(BF16)
        main = grads(query[:MAIN], key[:MAIN], value[:MAIN], grad[:MAIN], p_main[head])
        tail = grads(query[MAIN:], key[MAIN:], value[MAIN:], grad[MAIN:], p_tail[head])
        for i in range(3):
            qkv[i, :MAIN, lanes] = main[i].astype(BF16)
            qkv[i, MAIN:, lanes] = tail[i].astype(BF16)
        return 0

    lax.fori_loop(0, HEADS, backward, 0)
    store = pltpu.make_async_copy(qkv, grad_hbm, local.at[0])
    store.start()

    pass_on(3)
    finish_x(2)
    finish_x(3)

    for copy in y_copies:
        copy.wait_recv()
    for part in range(2):
        rows = slice(part * SHARD, part * SHARD + SHARD)
        term = y_own[3, rows, :].astype(F32)
        for k in range(3):
            term = term + y_in[k, rows, :].astype(F32)
        z_own[part] = term.astype(BF16)

    mine = (z_lo // 2) == core
    z_copies = []
    for k in range(1, 8):
        t = lax.rem(z + k, 8)
        to_lo, to_hi = t % 4, t // 4
        wide = pl.ds(pl.multiple_of(to_hi * 384, 128), 512)
        copy = remote(z_own.at[to_lo % 2, :, wide], z_in.at[k - 1], ZS + k - 1, at_z(k))
        goes = (to_lo // 2) == core
        pl.when(goes)(copy.start)
        z_copies.append((goes, copy))
    fin_copy = remote(total, total, FIN, sibling)

    @pl.when(mine)
    def _():
        for _, copy in z_copies:
            copy.wait_recv()
        wide = pl.ds(pl.multiple_of(z_hi * 384, 128), 512)
        term = z_own[z_lo % 2, :, wide].astype(F32)
        for k in range(7):
            term = term + z_in[k].astype(F32)
        total[...] = term
        fin_copy.start()
        fin_copy.wait_send()

    @pl.when(jnp.logical_not(mine))
    def _():
        fin_copy.wait_recv()

    proj_ref[...] = total[...]
    store.wait()
    for goes, copy in z_copies:
        pl.when(goes)(copy.wait_send)
    for copy in sent + y_copies + [c for hop in hops for c in hop]:
        copy.wait_send()


def local_part(query_key_value, cotangent, proj_weight, layer_scale, lengths):
    any_space = pl.BlockSpec(memory_space=pl.ANY)
    vmem = pl.BlockSpec(memory_space=pltpu.VMEM)
    grad, window = pl.pallas_call(
        kernel,
        out_shape=(
            jax.ShapeDtypeStruct((3, ROWS, HD), BF16),
            jax.ShapeDtypeStruct((SHARD, 512), F32),
        ),
        in_specs=[any_space, any_space, any_space, vmem, pl.BlockSpec(memory_space=pltpu.SMEM)],
        out_specs=(any_space, vmem),
        scratch_shapes=[
            pltpu.VMEM((3, ROWS, HD), BF16),
            pltpu.VMEM((2, ROWS, D), BF16),
            pltpu.VMEM((2, HD, ROWS), BF16),
            pltpu.VMEM((HEADS, MAIN, MAIN), F32),
            pltpu.VMEM((HEADS, TAIL, TAIL), F32),
            pltpu.VMEM((4, 4, SHARD, FIRST), BF16),
            pltpu.VMEM((4, 4, SHARD, LAST), BF16),
            pltpu.VMEM((HD, HALF), BF16),
            pltpu.VMEM((ROWS, HD), F32),
            pltpu.VMEM((ROWS, HD), BF16),
            pltpu.VMEM((ROWS, HD), BF16),
            pltpu.VMEM((4, 4, CHUNK, WIN), BF16),
            pltpu.VMEM((4, 3, CHUNK, WIN), BF16),
            pltpu.VMEM((4, CHUNK, WIN), BF16),
            pltpu.VMEM((3, CHUNK, WIN), BF16),
            pltpu.VMEM((2, SHARD, WIN), BF16),
            pltpu.VMEM((7, SHARD, 512), BF16),
            pltpu.VMEM((SHARD, 512), F32),
            pltpu.SemaphoreType.DMA((N_MSG,)),
            pltpu.SemaphoreType.DMA((N_MSG,)),
            pltpu.SemaphoreType.DMA((4,)),
        ],
        compiler_params=pltpu.CompilerParams(
            collective_id=0, has_side_effects=True, vmem_limit_bytes=62 * 2**20
        ),
        name="attention_block",
    )(query_key_value, cotangent, proj_weight, layer_scale.reshape(1, D), lengths.reshape(16, 4))
    dp = lax.axis_index("dp")
    start = (dp // 4) * 32 + ((dp // 2) % 2) * 16 + (dp % 2) * 200
    return grad, lax.dynamic_slice(window, (0, start), (SHARD, 200))


def solution(mesh):
    placed = (
        P(None, ("dp", "fsdp"), None),
        P(("dp", "fsdp"), None),
        P("fsdp", None),
        P(),
        P(None, "fsdp", None),
    )
    return jax.shard_map(
        local_part,
        mesh=mesh,
        in_specs=placed,
        out_specs=(P(None, ("dp", "fsdp"), None), P("fsdp", "dp")),
        check_vma=False,
    )
```

```python
import jax
import jax.numpy as jnp
from jax import lax
from jax.experimental import pallas as pl
from jax.experimental.pallas import tpu as pltpu
from jax.sharding import PartitionSpec as P

HS = 128
HEADS = 13
HD = HS * HEADS
D = 3200
MAIN = 256
SLOT = 96
TAIL = 2 * SLOT
ROWS = MAIN + TAIL
SHARD = HD // 16
HALF = 13 * 128
FIRST = 7 * 128
LAST = HALF - FIRST
WIN = 7 * 128
STEP = 6 * 128
CHUNK = 208
FACTOR = HS ** (-0.5)
LOG2E = 1.4426950408889634
MESH = pl.DeviceIdType.MESH
F32 = jnp.float32
BF16 = jnp.bfloat16

A1, B1, A2, A3, B2, B3 = 0, 3, 7, 9, 11, 13
COT, ATT, GRAD, XS, YS, ZS, FIN = 15, 20, 24, 25, 49, 55, 76
N_MSG = 77
PARTS = ((0, 512), (512, 384))


def dot_nn(a, b):
    return lax.dot_general(a, b, (((1,), (0,)), ((), ())), preferred_element_type=F32)


def dot_nt(a, b):
    return lax.dot_general(a, b, (((1,), (1,)), ((), ())), preferred_element_type=F32)


def dot_tn(a, b):
    return lax.dot_general(a, b, (((0,), (0,)), ((), ())), preferred_element_type=F32)


def kernel(
    qkv_hbm, cot_hbm, w_hbm, scale_hbm, lens_ref, grad_hbm, proj_ref,
    qkv, scaled, scale, att, bias_main, bias_tail, p_main, p_tail, w_a, w_b, w_all, go_own, go_out, go_in,
    xa_own, xb_own, xa_in, xb_in, ya_own, yb_own, ya_in, yb_in, za, zb, z_in, total, send, recv, local,
):
    dp, member = lax.axis_index("dp"), lax.axis_index("fsdp")
    x, z_hi, core = dp // 4, (dp // 2) % 2, dp % 2
    y, z_lo = member // 4, member % 4
    z = z_hi * 4 + z_lo

    def at_x(k):
        return (lax.rem(x + k, 4) * 4 + z_hi * 2 + core, member)

    def at_y(k):
        return (dp, lax.rem(y + k, 4) * 4 + z_lo)

    def at_z(k):
        t = lax.rem(z + k, 8)
        return (x * 4 + (t // 4) * 2 + core, y * 4 + t % 4)

    sibling = (x * 4 + z_hi * 2 + 1 - core, member)

    def remote(src, dst, index, device):
        return pltpu.make_async_remote_copy(
            src_ref=src, dst_ref=dst, send_sem=send.at[index], recv_sem=recv.at[index],
            device_id=device, device_id_type=MESH,
        )

    def launch(*args):
        copy = remote(*args)
        copy.start()
        return copy

    load_qkv = pltpu.make_async_copy(qkv_hbm, qkv, local.at[0])
    load_qkv.start()
    load_scale = pltpu.make_async_copy(scale_hbm, scale.at[0], local.at[4])
    load_scale.start()
    load_cot = pltpu.make_async_copy(cot_hbm, scaled.at[0], local.at[1])
    load_cot.start()

    col = pl.multiple_of(core * (12 * 128), 128)
    part_a = w_hbm.at[:, pl.ds(col, FIRST)]
    part_b = w_hbm.at[:, pl.ds(col + FIRST, LAST)]
    load_a = pltpu.make_async_copy(part_a, w_a.at[z_lo, y], local.at[2])
    load_a.start()
    load_b = pltpu.make_async_copy(part_b, w_b.at[y, z_lo], local.at[3])
    load_b.start()

    peers = [sibling, at_x(1), at_x(3)] + [at_y(k) for k in (1, 2, 3)] + [at_z(k) for k in range(1, 8)]
    barrier = pltpu.get_barrier_semaphore()
    for peer in peers:
        pl.semaphore_signal(barrier, inc=1, device_id=peer, device_id_type=MESH)
    pl.semaphore_wait(barrier, len(peers))

    windows = [pl.multiple_of(lax.rem(x + k, 4) * STEP, 128) for k in (2, 3, 1, 0)]
    pieces = [pl.ds(low, STEP) for low in windows] + [pl.ds(D - 128, 128)]
    cot_copies = [
        launch(cot_hbm.at[:, piece], scaled.at[1, :, piece], COT + i, sibling) for i, piece in enumerate(pieces)
    ]
    sent = list(cot_copies)

    gather_a = [launch(part_a, w_a.at[z_lo, y], A1 + i, at_y(k)) for i, k in enumerate((1, 3, 2))]
    small = LAST // 2
    gather_b = [launch(part_b, w_b.at[y, z_lo], B1 + i, at_z(k)) for i, k in enumerate((1, 7))]
    for i, k in enumerate((2, 6)):
        piece = w_hbm.at[:, pl.ds(col + FIRST + i * small, small)]
        gather_b.append(launch(piece, w_b.at[y, z_lo, :, pl.ds(i * small, small)], B1 + 2 + i, at_z(k)))
    sent += gather_a + gather_b

    first_count = lens_ref[dp, 0, 0]
    count_2, count_3 = lens_ref[dp, 0, 2], lens_ref[dp, 0, 3]

    def main_mask():
        rows = lax.broadcasted_iota(jnp.int32, (MAIN, MAIN), 0)
        cols = lax.broadcasted_iota(jnp.int32, (MAIN, MAIN), 1)
        one = jnp.where(rows >= first_count, 1, 0)
        two = jnp.where(cols >= first_count, 1, 0)
        return one == two

    def tail_mask():
        def ids(axis):
            at = lax.broadcasted_iota(jnp.int32, (TAIL, TAIL), axis)
            first = jnp.where(at < count_2, 2, -1)
            second = jnp.where(at - SLOT < count_3, 3, -1)
            return jnp.where(at < SLOT, first, second)

        one, two = ids(0), ids(1)
        return (one == two) & (one >= 0)

    bias_main[...] = jnp.where(main_mask(), 0.0, -1e30)
    bias_tail[...] = jnp.where(tail_mask(), 0.0, -1e30)

    def soft(query, key, bias):
        scores = dot_nt(query, key) * (FACTOR * LOG2E) + bias
        highest = jnp.maximum(jnp.max(scores, axis=1, keepdims=True), -1e29)
        weights = jnp.exp2(scores - highest)
        norm = jnp.sum(weights, axis=1, keepdims=True)
        return weights * (1.0 / jnp.where(norm > 0.0, norm, 1.0))

    load_qkv.wait()

    def forward(head, _):
        lanes = pl.ds(pl.multiple_of(head * HS, HS), HS)
        query, key, value = qkv[0, :, lanes], qkv[1, :, lanes], qkv[2, :, lanes]
        probs = soft(query[:MAIN], key[:MAIN], bias_main[...])
        probs_t = soft(query[MAIN:], key[MAIN:], bias_tail[...])
        p_main[head] = probs
        p_tail[head] = probs_t
        out = dot_nn(probs.astype(BF16), value[:MAIN])
        out_t = dot_nn(probs_t.astype(BF16), value[MAIN:])
        att[0, lanes, :] = jnp.concatenate([out, out_t], axis=0).T.astype(BF16)
        return 0

    att_copies = []

    def heads(i):
        block = lax.rem(y + 1 + i, 4)
        low, high = 3 * block, 3 * block + 4
        if i > 0:
            low = low + jnp.where(block > 0, 1, 0)
        if i == 3:
            high = high - jnp.where(block < 3, 1, 0)
        lax.fori_loop(low, high, forward, 0)
        rows = pl.ds(pl.multiple_of(416 * block + CHUNK * (1 - core), 16), CHUNK)
        att_copies.append(launch(att.at[0, rows], att.at[1, rows], ATT + i, sibling))

    def scale_piece(part, piece):
        def one(step, _):
            rows = pl.ds(pl.multiple_of(step * 64, 64), 64)
            scaled[part, rows, piece] = (scaled[part, rows, piece].astype(F32) * scale[:, piece]).astype(BF16)
            return 0

        lax.fori_loop(0, ROWS // 64, one, 0)

    x_own, x_in = (xa_own, xb_own), (xa_in, xb_in)
    y_own, y_in = (ya_own, yb_own), (ya_in, yb_in)
    hops, y_copies, z_copies = [], ([], []), []

    def way_of(i):
        return 1 if i % 2 == 0 else 3

    def multiply(i):
        part, at = i // 4, i % 4
        way = way_of(i)
        rows = pl.ds(pl.multiple_of(416 * lax.rem(y + 1 + at, 4) + CHUNK * core, 16), CHUNK)
        if part == 0:
            att_copies[at].wait_recv()
        hop = []
        low, size = PARTS[part]
        order = (2, 4 - way, way, 0)
        for j, k in enumerate(order):
            if i == 0:
                scale_piece(0, pieces[j])
                cot_copies[j].wait_recv()
                scale_piece(1, pieces[j])
            cols = pl.ds(pl.multiple_of(lax.rem(x + k, 4) * STEP + low, 128), size)
            term = dot_nn(att[0, rows, :], scaled[0, :, cols]) + dot_nn(att[1, rows, :], scaled[1, :, cols])
            x_own[part][at, j] = term.astype(BF16)
            if j < 2:
                to = at_x(way if j == 0 else 4 - way)
                hop.append(launch(x_own[part].at[at, j], x_in[part].at[at, j], XS + 3 * i + j, to))
        hops.append(hop)

    def pass_on(i):
        part, at = i // 4, i % 4
        own, came = x_own[part], x_in[part]
        hops[i][0].wait_recv()

        def add(step, _):
            rows = pl.ds(pl.multiple_of(step * 16, 16), 16)
            own[at, 2, rows, :] = (own[at, 2, rows, :].astype(F32) + came[at, 0, rows, :].astype(F32)).astype(BF16)
            return 0

        lax.fori_loop(0, CHUNK // 16, add, 0)
        hops[i].append(launch(own.at[at, 2], came.at[at, 2], XS + 3 * i + 2, at_x(way_of(i))))

    def finish_x(i):
        part, at = i // 4, i % 4
        own, came, out = x_own[part], x_in[part], y_own[part]
        hops[i][1].wait_recv()
        hops[i][2].wait_recv()

        def add(step, _):
            rows = pl.ds(pl.multiple_of(step * 16, 16), 16)
            term = own[at, 3, rows, :].astype(F32) + came[at, 1, rows, :].astype(F32) + came[at, 2, rows, :].astype(F32)
            out[at, rows, :] = term.astype(BF16)
            return 0

        lax.fori_loop(0, CHUNK // 16, add, 0)
        if at < 3:
            y_copies[part].append(launch(out.at[at], y_in[part].at[at], YS + 3 * part + at, at_y(1 + at)))

    def finish_y(part):
        out = (za, zb)[part]
        for copy in y_copies[part]:
            copy.wait_recv()
        for half in range(2):
            rows = slice(half * SHARD, half * SHARD + SHARD)
            term = y_own[part][3, rows, :].astype(F32)
            for k in range(3):
                term = term + y_in[part][k, rows, :].astype(F32)
            out[half] = term.astype(BF16)
        for k in range(1, 8):
            t = lax.rem(z + k, 8)
            to_lo, to_hi = t % 4, t // 4
            goes = (to_lo // 2) == core
            low, high = goes & (to_hi == 0), goes & (to_hi == 1)
            if part == 0:
                todo = [
                    (low, mine & (z_hi == 0), za.at[to_lo % 2], z_in.at[k - 1], ZS + k - 1),
                    (high, mine & (z_hi == 1), za.at[to_lo % 2, :, pl.ds(384, 128)], z_in.at[k - 1, :, pl.ds(0, 128)], ZS + 6 + k),
                ]
            else:
                todo = [(high, mine & (z_hi == 1), zb.at[to_lo % 2], z_in.at[k - 1, :, pl.ds(128, 384)], ZS + 13 + k)]
            for goes_now, comes, src, dst, index in todo:
                copy = remote(src, dst, index, at_z(k))
                pl.when(goes_now)(copy.start)
                z_copies.append((goes_now, comes, copy))

    mine = (z_lo // 2) == core

    heads(0)
    load_scale.wait()
    load_cot.wait()
    multiply(0)
    heads(1)

    load_a.wait()
    load_b.wait()
    for copy in gather_a:
        copy.wait_recv()
    wide_a = [launch(w_a.at[z_lo], w_a.at[z_lo], A2 + i, at_z(k)) for i, k in enumerate((1, 7))]
    for copy in gather_b:
        copy.wait_recv()
    wide_b = [launch(w_b.at[y], w_b.at[y], B2 + i, at_y(k)) for i, k in enumerate((1, 3))]
    sent += wide_a + wide_b

    multiply(1)
    pass_on(0)
    heads(2)
    multiply(2)
    pass_on(1)
    heads(3)
    multiply(3)
    pass_on(2)

    wide_a[0].wait_recv()
    behind, ahead = lax.rem(z_lo + 3, 4), lax.rem(z_lo + 1, 4)
    far_a = [launch(w_a.at[behind, pl.ds(0, 2)], w_a.at[behind, pl.ds(0, 2)], A3, at_z(1))]
    wide_a[1].wait_recv()
    far_a.append(launch(w_a.at[ahead, pl.ds(2, 2)], w_a.at[ahead, pl.ds(2, 2)], A3 + 1, at_z(7)))
    behind, ahead = lax.rem(y + 3, 4), lax.rem(y + 1, 4)
    wide_b[0].wait_recv()
    far_b = [launch(w_b.at[behind, pl.ds(0, 2)], w_b.at[behind, pl.ds(0, 2)], B3, at_y(1))]
    wide_b[1].wait_recv()
    far_b.append(launch(w_b.at[ahead, pl.ds(2, 2)], w_b.at[ahead, pl.ds(2, 2)], B3 + 1, at_y(3)))
    sent += far_a + far_b

    cot_copies[4].wait_recv()
    scale_piece(0, pieces[4])
    scale_piece(1, pieces[4])
    multiply(4)
    pass_on(3)
    multiply(5)
    finish_x(0)
    finish_x(1)
    for copy in far_a + far_b:
        copy.wait_recv()

    for block in range(4):
        rows = slice(416 * block, 416 * block + 416)
        left = jnp.concatenate([w_a[k, block].astype(F32) for k in range(4)], axis=0)
        w_all[rows, :FIRST] = left.astype(BF16)
        right = jnp.concatenate([w_b[block, k].astype(F32) for k in range(4)], axis=0)
        w_all[rows, FIRST:] = right.astype(BF16)

    keep = jnp.where(core == 1, 0.0, 1.0)
    w_all[:, :128] = (w_all[:, :128].astype(F32) * keep).astype(BF16)

    pass_on(4)
    multiply(6)

    cols = pl.ds(col, HALF)
    cuts = ((0, 512), (512, 512), (1024, 640))
    for low, size in cuts:
        go_out[:, low:low + size] = dot_nt(scaled[1, :, cols], w_all[low:low + size, :]).astype(BF16)
    go_copy = launch(go_out, go_in, GRAD, sibling)
    sent.append(go_copy)
    pass_on(5)
    multiply(7)
    finish_x(2)
    for low, size in cuts:
        go_own[:, low:low + size] = dot_nt(scaled[0, :, cols], w_all[low:low + size, :])
    pass_on(6)
    finish_x(3)
    finish_y(0)
    pass_on(7)
    go_copy.wait_recv()

    def grads(query, key, value, grad, probs):
        dprob = dot_nt(grad, value)
        delta = jnp.sum(probs * dprob, axis=1, keepdims=True)
        dscore = (probs * (dprob - delta) * FACTOR).astype(BF16)
        return dot_nn(dscore, key), dot_tn(dscore, query), dot_tn(probs.astype(BF16), grad)

    def backward(head, _):
        lanes = pl.ds(pl.multiple_of(head * HS, HS), HS)
        query, key, value = qkv[0, :, lanes], qkv[1, :, lanes], qkv[2, :, lanes]
        grad = (go_own[:, lanes] + go_in[:, lanes].astype(F32)).astype(BF16)
        main = grads(query[:MAIN], key[:MAIN], value[:MAIN], grad[:MAIN], p_main[head])
        tail = grads(query[MAIN:], key[MAIN:], value[MAIN:], grad[MAIN:], p_tail[head])
        for i in range(3):
            qkv[i, :MAIN, lanes] = main[i].astype(BF16)
            qkv[i, MAIN:, lanes] = tail[i].astype(BF16)
        return 0

    stores = []

    def back(low, high):
        lax.fori_loop(low, high, backward, 0)
        lanes = pl.ds(low * HS, (high - low) * HS)
        copy = pltpu.make_async_copy(qkv.at[:, :, lanes], grad_hbm.at[:, :, lanes], local.at[5 + len(stores)])
        copy.start()
        stores.append(copy)

    back(0, 4)
    finish_x(4)
    finish_x(5)
    back(4, 8)
    finish_x(6)
    finish_x(7)
    finish_y(1)
    back(8, HEADS)

    fin_copy = remote(total, total, FIN, sibling)
    for _, comes, copy in z_copies:
        pl.when(comes)(copy.wait_recv)

    def sum_z(term):
        for k in range(7):
            term = term + z_in[k].astype(F32)
        total[...] = term
        fin_copy.start()
        fin_copy.wait_send()

    @pl.when(mine & (z_hi == 0))
    def _():
        sum_z(za[z_lo % 2].astype(F32))

    @pl.when(mine & (z_hi == 1))
    def _():
        sum_z(jnp.concatenate([za[z_lo % 2, :, 384:], zb[z_lo % 2]], axis=1).astype(F32))

    @pl.when(jnp.logical_not(mine))
    def _():
        fin_copy.wait_recv()

    proj_ref[...] = total[...].T
    for copy in stores:
        copy.wait()
    for goes, _, copy in z_copies:
        pl.when(goes)(copy.wait_send)
    for copy in sent + att_copies + y_copies[0] + y_copies[1] + [c for hop in hops for c in hop]:
        copy.wait_send()


def local_part(query_key_value, cotangent, proj_weight, layer_scale, lengths):
    any_space = pl.BlockSpec(memory_space=pl.ANY)
    vmem = pl.BlockSpec(memory_space=pltpu.VMEM)
    grad, window = pl.pallas_call(
        kernel,
        out_shape=(
            jax.ShapeDtypeStruct((3, ROWS, HD), BF16),
            jax.ShapeDtypeStruct((512, SHARD), F32),
        ),
        in_specs=[any_space, any_space, any_space, any_space, pl.BlockSpec(memory_space=pltpu.SMEM)],
        out_specs=(any_space, vmem),
        scratch_shapes=[
            pltpu.VMEM((3, ROWS, HD), BF16),
            pltpu.VMEM((2, ROWS, D), BF16),
            pltpu.VMEM((1, D), F32),
            pltpu.VMEM((2, HD, ROWS), BF16),
            pltpu.VMEM((MAIN, MAIN), F32),
            pltpu.VMEM((TAIL, TAIL), F32),
            pltpu.VMEM((HEADS, MAIN, MAIN), F32),
            pltpu.VMEM((HEADS, TAIL, TAIL), F32),
            pltpu.VMEM((4, 4, SHARD, FIRST), BF16),
            pltpu.VMEM((4, 4, SHARD, LAST), BF16),
            pltpu.VMEM((HD, HALF), BF16),
            pltpu.VMEM((ROWS, HD), F32),
            pltpu.VMEM((ROWS, HD), BF16),
            pltpu.VMEM((ROWS, HD), BF16),
            pltpu.VMEM((4, 4, CHUNK, 512), BF16),
            pltpu.VMEM((4, 4, CHUNK, 384), BF16),
            pltpu.VMEM((4, 3, CHUNK, 512), BF16),
            pltpu.VMEM((4, 3, CHUNK, 384), BF16),
            pltpu.VMEM((4, CHUNK, 512), BF16),
            pltpu.VMEM((4, CHUNK, 384), BF16),
            pltpu.VMEM((3, CHUNK, 512), BF16),
            pltpu.VMEM((3, CHUNK, 384), BF16),
            pltpu.VMEM((2, SHARD, 512), BF16),
            pltpu.VMEM((2, SHARD, 384), BF16),
            pltpu.VMEM((7, SHARD, 512), BF16),
            pltpu.VMEM((SHARD, 512), F32),
            pltpu.SemaphoreType.DMA((N_MSG,)),
            pltpu.SemaphoreType.DMA((N_MSG,)),
            pltpu.SemaphoreType.DMA((8,)),
        ],
        compiler_params=pltpu.CompilerParams(
            collective_id=0, has_side_effects=True, vmem_limit_bytes=62 * 2**20
        ),
        name="attention_block",
    )(query_key_value, cotangent, proj_weight, layer_scale, lengths)
    dp = lax.axis_index("dp")
    start = (dp // 4) * 32 + ((dp // 2) % 2) * 16 + (dp % 2) * 200
    return grad, lax.dynamic_slice(window, (start, 0), (200, SHARD)).T


def solution(mesh):
    placed = (
        P(None, ("dp", "fsdp"), None),
        P(("dp", "fsdp"), None),
        P("fsdp", None),
        P(),
        P(None, "fsdp", None),
    )
    return jax.shard_map(
        local_part,
        mesh=mesh,
        in_specs=placed,
        out_specs=(P(None, ("dp", "fsdp"), None), P("fsdp", "dp")),
        check_vma=False,
    )
```

```python
import jax
import jax.numpy as jnp
from jax import lax
from jax.experimental import pallas as pl
from jax.experimental.pallas import tpu as pltpu
from jax.sharding import PartitionSpec as P

HS = 128
HEADS = 13
HD = HS * HEADS
D = 3200
MAIN = 256
SLOT = 96
TAIL = 2 * SLOT
ROWS = MAIN + TAIL
SHARD = HD // 16
HALF = 13 * 128
FIRST = 6 * 128
LAST = HALF - FIRST
STEP = 6 * 128
SEAM = 5 * 128
CHUNK = 208
FACTOR = HS ** (-0.5)
LOG2E = 1.4426950408889634
MESH = pl.DeviceIdType.MESH
F32 = jnp.float32
BF16 = jnp.bfloat16

A1, B1 = 0, 3
COT, ATT, GRAD, XS, YS, ZS, FIN = 15, 20, 24, 25, 49, 55, 76
SZ, SY, SX = 77, 89, 92
A2, A3, B2, B3 = 99, 107, 111, 119
N_MSG = 123
PARTS = ((128, 384), (512, 256))


def dot_nn(a, b):
    return lax.dot_general(a, b, (((1,), (0,)), ((), ())), preferred_element_type=F32)


def dot_nt(a, b):
    return lax.dot_general(a, b, (((1,), (1,)), ((), ())), preferred_element_type=F32)


def dot_tn(a, b):
    return lax.dot_general(a, b, (((0,), (0,)), ((), ())), preferred_element_type=F32)


def kernel(
    qkv_hbm, cot_hbm, w_hbm, scale_hbm, lens_ref, grad_hbm, proj_ref,
    qkv, scaled, scale, att, bias_main, bias_tail, p_main, p_tail, w_a, w_b, w_all, go_own, go_out, go_in,
    xa_own, xb_own, xa_in, xb_in, ya_own, yb_own, ya_in, yb_in, za, zb, z_in, total,
    turned, seam, sz_own, sz_in, sy_own, sy_in, sx_own, sx_in, send, recv, local,
):
    dp, member = lax.axis_index("dp"), lax.axis_index("fsdp")
    x, z_hi, core = dp // 4, (dp // 2) % 2, dp % 2
    y, z_lo = member // 4, member % 4
    z = z_hi * 4 + z_lo

    def at_x(k):
        return (lax.rem(x + k, 4) * 4 + z_hi * 2 + core, member)

    def at_y(k):
        return (dp, lax.rem(y + k, 4) * 4 + z_lo)

    def at_xz(k, flip):
        return (lax.rem(x + k, 4) * 4 + (z_hi + flip) % 2 * 2 + core, member)

    def at_z(k):
        t = lax.rem(z + k, 8)
        return (x * 4 + (t // 4) * 2 + core, y * 4 + t % 4)

    sibling = (x * 4 + z_hi * 2 + 1 - core, member)

    def remote(src, dst, index, device):
        return pltpu.make_async_remote_copy(
            src_ref=src, dst_ref=dst, send_sem=send.at[index], recv_sem=recv.at[index],
            device_id=device, device_id_type=MESH,
        )

    def launch(*args):
        copy = remote(*args)
        copy.start()
        return copy

    first = lax.rem(y + 1, 4)

    def load_heads(low, count, index):
        lanes = pl.ds(pl.multiple_of(low * HS, HS), count * HS)
        copy = pltpu.make_async_copy(qkv_hbm.at[:, :, lanes], qkv.at[:, :, lanes], local.at[index])
        copy.start()
        return copy

    loads = [load_heads(3 * first, 3, 8), load_heads(12, 1, 9)]
    loads += [load_heads(3 * lax.rem(first + k, 4), 3, 9 + k) for k in (1, 2, 3)]
    load_scale = pltpu.make_async_copy(scale_hbm, scale.at[0], local.at[4])
    load_scale.start()
    load_cot = pltpu.make_async_copy(cot_hbm, scaled.at[0], local.at[1])
    load_cot.start()

    col = pl.multiple_of(core * (12 * 128), 128)
    part_a = w_hbm.at[:, pl.ds(col, FIRST)]
    part_b = w_hbm.at[:, pl.ds(col + FIRST, LAST)]
    load_a = pltpu.make_async_copy(part_a, w_a.at[z_lo, y], local.at[2])
    load_a.start()
    load_b = pltpu.make_async_copy(part_b, w_b.at[y, z_lo], local.at[3])
    load_b.start()

    peers = [sibling, at_x(1), at_x(3)] + [at_y(k) for k in (1, 2, 3)] + [at_z(k) for k in range(1, 8)]
    peers += [at_x(2)] + [at_xz(k, 1) for k in (1, 2, 3)]
    barrier = pltpu.get_barrier_semaphore()
    for peer in peers:
        pl.semaphore_signal(barrier, inc=1, device_id=peer, device_id_type=MESH)
    first_count = lens_ref[dp, 0, 0]
    count_2, count_3 = lens_ref[dp, 0, 2], lens_ref[dp, 0, 3]

    def main_mask():
        rows = lax.broadcasted_iota(jnp.int32, (MAIN, MAIN), 0)
        cols = lax.broadcasted_iota(jnp.int32, (MAIN, MAIN), 1)
        one = jnp.where(rows >= first_count, 1, 0)
        two = jnp.where(cols >= first_count, 1, 0)
        return one == two

    def tail_mask():
        def ids(axis):
            at = lax.broadcasted_iota(jnp.int32, (TAIL, TAIL), axis)
            first = jnp.where(at < count_2, 2, -1)
            second = jnp.where(at - SLOT < count_3, 3, -1)
            return jnp.where(at < SLOT, first, second)

        one, two = ids(0), ids(1)
        return (one == two) & (one >= 0)

    bias_main[...] = jnp.where(main_mask(), 0.0, -1e30)
    bias_tail[...] = jnp.where(tail_mask(), 0.0, -1e30)

    def soft(query, key, bias):
        scores = dot_nt(query, key) * (FACTOR * LOG2E) + bias
        highest = jnp.maximum(jnp.max(scores, axis=1, keepdims=True), -1e29)
        weights = jnp.exp2(scores - highest)
        norm = jnp.sum(weights, axis=1, keepdims=True)
        return weights * (1.0 / jnp.where(norm > 0.0, norm, 1.0))

    def forward(head):
        lanes = pl.ds(pl.multiple_of(head * HS, HS), HS)
        query, key, value = qkv[0, :, lanes], qkv[1, :, lanes], qkv[2, :, lanes]
        probs = soft(query[:MAIN], key[:MAIN], bias_main[...])
        probs_t = soft(query[MAIN:], key[MAIN:], bias_tail[...])
        p_main[head] = probs
        p_tail[head] = probs_t
        out = dot_nn(probs.astype(BF16), value[:MAIN])
        out_t = dot_nn(probs_t.astype(BF16), value[MAIN:])
        att[0, lanes, :] = jnp.concatenate([out, out_t], axis=0).T.astype(BF16)

    for copy in loads[:3]:
        copy.wait()
    forward(3 * first)
    forward(3 * first + 1)
    pl.semaphore_wait(barrier, len(peers))

    windows = [pl.multiple_of(lax.rem(x + k, 4) * STEP, 128) for k in (2, 3, 1, 0)]
    pieces = [pl.ds(low, STEP) for low in windows] + [pl.ds(D - 128, 128)]
    cot_copies = []

    def send_cot(low, high):
        for i in range(low, high):
            piece = pieces[i]
            cot_copies.append(launch(cot_hbm.at[:, piece], scaled.at[1, :, piece], COT + i, sibling))

    send_cot(0, 2)
    sent = []

    gather_a = [launch(part_a, w_a.at[z_lo, y], A1 + i, at_y(k)) for i, k in enumerate((1, 3, 2))]
    gather_b = [launch(part_b, w_b.at[y, z_lo], B1 + i, at_z(k)) for i, k in enumerate((1, 7))]
    for i, (k, low, size) in enumerate(((2, 0, 512), (6, 512, 384))):
        piece = w_hbm.at[:, pl.ds(col + FIRST + low, size)]
        gather_b.append(launch(piece, w_b.at[y, z_lo, :, pl.ds(low, size)], B1 + 2 + i, at_z(k)))
    shards_a = [w_a.at[z_lo, lax.rem(y + k, 4)] for k in (0, 3, 1, 2)]
    shards_b = [w_b.at[y, lax.rem(z_lo + k, 4)] for k in (0, 3, 1, 2)]
    wide_a = [[launch(part_a, shards_a[0], A2 + 4 * i, at_z((1, 7)[i]))] for i in range(2)]
    wide_b = [[launch(part_b, shards_b[0], B2 + 4 * i, at_y((1, 3)[i]))] for i in range(2)]
    sent += gather_a + gather_b

    att_copies = []

    def heads(i):
        block = lax.rem(y + 1 + i, 4)
        low, high = 3 * block, 3 * block + 4
        if i == 0:
            low = low + 2
        else:
            low = low + jnp.where(block > 0, 1, 0)
        if i == 3:
            high = high - jnp.where(block < 3, 1, 0)

        def pair(step, _):
            forward(low + 2 * step)
            forward(jnp.minimum(low + 2 * step + 1, high - 1))
            return 0

        lax.fori_loop(0, (high - low + 1) // 2, pair, 0)
        rows = pl.ds(pl.multiple_of(416 * block + CHUNK * (1 - core), 16), CHUNK)
        att_copies.append(launch(att.at[0, rows], att.at[1, rows], ATT + i, sibling))
        if i == 0:
            send_cot(2, 5)

    def scale_piece(part, piece):
        def one(step, _):
            rows = pl.ds(pl.multiple_of(step * 64, 64), 64)
            scaled[part, rows, piece] = (scaled[part, rows, piece].astype(F32) * scale[:, piece]).astype(BF16)
            return 0

        lax.fori_loop(0, ROWS // 64, one, 0)

    x_own, x_in = (xa_own, xb_own), (xa_in, xb_in)
    y_own, y_in = (ya_own, yb_own), (ya_in, yb_in)
    hops, y_copies, z_copies = [], ([], []), []

    def way_of(i):
        return 1 if i % 2 == 0 else 3

    def multiply(i):
        part, at = i // 4, i % 4
        way = way_of(i)
        rows = pl.ds(pl.multiple_of(416 * lax.rem(y + 1 + at, 4) + CHUNK * core, 16), CHUNK)
        if i == 0:
            for j in range(4):
                scale_piece(0, pieces[j])
        if part == 0:
            att_copies[at].wait_recv()
        hop = []
        low, size = PARTS[part]
        order = (2, 4 - way, way, 0)
        for j, k in enumerate(order):
            if i == 0:
                cot_copies[j].wait_recv()
                scale_piece(1, pieces[j])
            cols = pl.ds(pl.multiple_of(lax.rem(x + k, 4) * STEP + low, 128), size)
            term = dot_nn(att[0, rows, :], scaled[0, :, cols]) + dot_nn(att[1, rows, :], scaled[1, :, cols])
            x_own[part][at, j] = term.astype(BF16)
            if j < 2:
                to = at_x(way if j == 0 else 4 - way)
                hop.append(launch(x_own[part].at[at, j], x_in[part].at[at, j], XS + 3 * i + j, to))
        hops.append(hop)

    def pass_on(i):
        part, at = i // 4, i % 4
        own, came = x_own[part], x_in[part]
        hops[i][0].wait_recv()

        def add(step, _):
            rows = pl.ds(pl.multiple_of(step * 16, 16), 16)
            own[at, 2, rows, :] = (own[at, 2, rows, :].astype(F32) + came[at, 0, rows, :].astype(F32)).astype(BF16)
            return 0

        lax.fori_loop(0, CHUNK // 16, add, 0)
        hops[i].append(launch(own.at[at, 2], came.at[at, 2], XS + 3 * i + 2, at_x(way_of(i))))

    def finish_x(i):
        part, at = i // 4, i % 4
        own, came, out = x_own[part], x_in[part], y_own[part]
        hops[i][1].wait_recv()
        hops[i][2].wait_recv()

        def add(step, _):
            rows = pl.ds(pl.multiple_of(step * 16, 16), 16)
            term = own[at, 3, rows, :].astype(F32) + came[at, 1, rows, :].astype(F32) + came[at, 2, rows, :].astype(F32)
            out[at, rows, :] = term.astype(BF16)
            return 0

        lax.fori_loop(0, CHUNK // 16, add, 0)
        if at < 3:
            y_copies[part].append(launch(out.at[at], y_in[part].at[at], YS + 3 * part + at, at_y(1 + at)))

    def finish_y(part):
        out = (za, zb)[part]
        for copy in y_copies[part]:
            copy.wait_recv()
        for half in range(2):
            rows = slice(half * SHARD, half * SHARD + SHARD)
            term = y_own[part][3, rows, :].astype(F32)
            for k in range(3):
                term = term + y_in[part][k, rows, :].astype(F32)
            out[half] = term.astype(BF16)
        for k in range(1, 8):
            t = lax.rem(z + k, 8)
            to_lo, to_hi = t % 4, t // 4
            goes = (to_lo // 2) == core
            low, high = goes & (to_hi == 0), goes & (to_hi == 1)
            if part == 0:
                todo = [
                    (low, mine & (z_hi == 0), za.at[to_lo % 2], z_in.at[k - 1], ZS + k - 1),
                    (high, mine & (z_hi == 1), za.at[to_lo % 2, :, pl.ds(256, 128)], z_in.at[k - 1, :, pl.ds(0, 128)], ZS + 6 + k),
                ]
            else:
                todo = [(high, mine & (z_hi == 1), zb.at[to_lo % 2], z_in.at[k - 1, :, pl.ds(128, 256)], ZS + 13 + k)]
            for goes_now, comes, src, dst, index in todo:
                copy = remote(src, dst, index, at_z(k))
                pl.when(goes_now)(copy.start)
                z_copies.append((goes_now, comes, copy))

    mine = (z_lo // 2) == core

    seam_sends, seam_comes, seam_y, seam_x = [], [[] for _ in range(4)], [], []

    def gather_seam():
        for part in range(2):
            for k in range(5):
                seam[part, :, k * 128:k * 128 + 128] = scaled[part, :, k * STEP:k * STEP + 128]

    def seam_multiply(i):
        rows = pl.ds(pl.multiple_of(416 * lax.rem(y + 1 + i, 4) + CHUNK * core, 16), CHUNK)
        term = dot_nn(att[0, rows, :], seam[0]) + dot_nn(att[1, rows, :], seam[1])
        for half in range(2):
            sz_own[i, half] = term[half * SHARD:half * SHARD + SHARD].astype(BF16)
        for d in (1, 2, 3):
            to_lo = lax.rem(z_lo + d, 4)
            goes = (to_lo // 2) == core
            hop = (1, 2 if i < 2 else 6, 7)[d - 1]
            copy = remote(sz_own.at[i, to_lo % 2], sz_in.at[i, d - 1], SZ + 3 * i + d - 1, at_z(hop))
            pl.when(goes)(copy.start)
            seam_sends.append((goes, copy))
            seam_comes[i].append(copy)

    def seam_to_y(i):
        @pl.when(mine)
        def _():
            for copy in seam_comes[i]:
                copy.wait_recv()
            term = sz_own[i, z_lo % 2].astype(F32)
            for k in range(3):
                term = term + sz_in[i, k].astype(F32)
            sy_own[i] = term.astype(BF16)

        if i < 3:
            copy = remote(sy_own.at[i], sy_in.at[i], SY + i, at_y(1 + i))
            pl.when(mine)(copy.start)
            seam_y.append(copy)

    def seam_to_x():
        @pl.when(mine)
        def _():
            term = sy_own[3].astype(F32)
            for k in range(3):
                seam_y[k].wait_recv()
                term = term + sy_in[k].astype(F32)
            sx_own[...] = term.astype(BF16)

        for k in range(1, 8):
            to_x, flip = lax.rem(x + k // 2, 4), k % 2
            group = to_x + (z_hi + flip) % 2
            src = sx_own.at[:, pl.ds(pl.multiple_of(group * 128, 128), 128)]
            copy = remote(src, sx_in.at[k - 1], SX + k - 1, at_xz(k // 2, flip))
            pl.when(mine)(copy.start)
            seam_x.append(copy)

    def widen(j):
        if j == 1:
            load_a.wait()
            load_b.wait()
        gather_a[j - 1].wait_recv()
        gather_b[j - 1].wait_recv()
        if j == 3:
            gather_b[3].wait_recv()
        for i in range(2):
            wide_a[i].append(launch(shards_a[j], shards_a[j], A2 + 4 * i + j, at_z((1, 7)[i])))
            wide_b[i].append(launch(shards_b[j], shards_b[j], B2 + 4 * i + j, at_y((1, 3)[i])))

    far_copies = []

    def far(j):
        i = j // 2
        wide_a[i][j].wait_recv()
        wide_b[i][j].wait_recv()
        shard = w_a.at[lax.rem(z_lo + (3, 1)[i], 4), lax.rem(y + (0, 3, 1, 2)[j], 4)]
        far_copies.append(launch(shard, shard, A3 + j, at_z((1, 7)[i])))
        shard = w_b.at[lax.rem(y + (3, 1)[i], 4), lax.rem(z_lo + (0, 3, 1, 2)[j], 4)]
        far_copies.append(launch(shard, shard, B3 + j, at_y((1, 3)[i])))

    def last_piece():
        cot_copies[4].wait_recv()
        scale_piece(0, pieces[4])
        scale_piece(1, pieces[4])
        gather_seam()

    def collect():
        for j in (0, 1):
            wide_a[1][j].wait_recv()
            wide_b[1][j].wait_recv()
            wide_a[0][j + 2].wait_recv()
            wide_b[0][j + 2].wait_recv()
        for copy in far_copies:
            copy.wait_recv()

        for block in range(4):
            rows = slice(416 * block, 416 * block + 416)
            left = jnp.concatenate([w_a[k, block].astype(F32) for k in range(4)], axis=0)
            w_all[rows, :FIRST] = left.astype(BF16)
            right = jnp.concatenate([w_b[block, k].astype(F32) for k in range(4)], axis=0)
            w_all[rows, FIRST:] = right.astype(BF16)

        keep = jnp.where(core == 1, 0.0, 1.0)
        w_all[:, :128] = (w_all[:, :128].astype(F32) * keep).astype(BF16)

    def grad_out(part):
        cols = pl.ds(col, HALF)
        for low, size in ((0, 512), (512, 512), (1024, 640)):
            term = dot_nt(scaled[part, :, cols], w_all[low:low + size, :])
            if part == 1:
                go_out[:, low:low + size] = term.astype(BF16)
            else:
                go_own[:, low:low + size] = term

    def grads(query, key, value, grad, probs):
        dprob = dot_nt(grad, value)
        delta = jnp.sum(probs * dprob, axis=1, keepdims=True)
        dscore = (probs * (dprob - delta) * FACTOR).astype(BF16)
        return dot_nn(dscore, key), dot_tn(dscore, query), dot_tn(probs.astype(BF16), grad)

    def backward(head):
        lanes = pl.ds(pl.multiple_of(head * HS, HS), HS)
        query, key, value = qkv[0, :, lanes], qkv[1, :, lanes], qkv[2, :, lanes]
        grad = (go_own[:, lanes] + go_in[:, lanes].astype(F32)).astype(BF16)
        main = grads(query[:MAIN], key[:MAIN], value[:MAIN], grad[:MAIN], p_main[head])
        tail = grads(query[MAIN:], key[MAIN:], value[MAIN:], grad[MAIN:], p_tail[head])
        for i in range(3):
            qkv[i, :MAIN, lanes] = main[i].astype(BF16)
            qkv[i, MAIN:, lanes] = tail[i].astype(BF16)

    stores = []

    def back(low, high):
        def pair(step, _):
            backward(low + 2 * step)
            backward(low + 2 * step + 1)
            return 0

        lax.fori_loop(0, (high - low) // 2, pair, 0)
        if (high - low) % 2:
            backward(high - 1)
        lanes = pl.ds(low * HS, (high - low) * HS)
        copy = pltpu.make_async_copy(qkv.at[:, :, lanes], grad_hbm.at[:, :, lanes], local.at[13 + len(stores)])
        copy.start()
        stores.append(copy)

    heads(0)
    for copy in loads[3:]:
        copy.wait()
    load_scale.wait()
    load_cot.wait()
    heads(1)
    multiply(0)
    widen(1)
    multiply(1)
    heads(2)
    pass_on(0)
    heads(3)
    multiply(2)
    far(0)
    widen(2)
    last_piece()
    multiply(3)
    multiply(4)
    widen(3)
    far(1)
    pass_on(2)
    multiply(5)
    pass_on(1)
    far(2)
    far(3)
    pass_on(5)
    seam_multiply(0)
    seam_multiply(1)
    pass_on(4)
    pass_on(3)
    seam_multiply(2)
    multiply(6)
    finish_x(1)
    multiply(7)
    finish_x(2)
    seam_multiply(3)
    finish_x(0)
    finish_x(5)
    collect()
    grad_out(1)
    go_copy = launch(go_out, go_in, GRAD, sibling)
    finish_x(3)
    seam_to_y(0)
    pass_on(6)
    finish_x(4)
    grad_out(0)
    go_copy.wait_recv()
    seam_to_y(1)
    pass_on(7)
    seam_to_y(2)
    finish_x(6)
    finish_y(0)
    back(0, 4)
    seam_to_y(3)
    back(4, 6)
    seam_to_x()
    finish_x(7)
    finish_y(1)
    back(6, 12)
    back(12, 13)

    fin_copy = remote(total, total, FIN, sibling)
    for _, comes, copy in z_copies:
        pl.when(comes)(copy.wait_recv)
    for copy in seam_x:
        pl.when(mine)(copy.wait_recv)

    def sum_seam():
        term = sx_own[:, pl.ds(pl.multiple_of((x + z_hi) * 128, 128), 128)].astype(F32)
        for k in range(7):
            term = term + sx_in[k].astype(F32)
        return term

    def sum_z(term, low, high):
        for k in range(7):
            term = term + z_in[k].astype(F32)
        total[:, low:high] = term
        fin_copy.start()
        fin_copy.wait_send()

    @pl.when(mine & (z_hi == 0))
    def _():
        total[:, :128] = sum_seam()
        sum_z(za[z_lo % 2].astype(F32), 128, 512)

    @pl.when(mine & (z_hi == 1))
    def _():
        total[:, 384:] = sum_seam()
        sum_z(jnp.concatenate([za[z_lo % 2, :, 256:], zb[z_lo % 2]], axis=1).astype(F32), 0, 384)

    @pl.when(jnp.logical_not(mine))
    def _():
        fin_copy.wait_recv()

    turned[...] = total[...].T
    start = x * 32 + z_hi * 16 + core * 200
    proj_ref[...] = turned[pl.ds(pl.multiple_of(start, 8), 200), :]
    for copy in stores:
        copy.wait()
    for goes, _, copy in z_copies:
        pl.when(goes)(copy.wait_send)
    for goes, copy in seam_sends:
        pl.when(goes)(copy.wait_send)
    for copy in seam_y + seam_x:
        pl.when(mine)(copy.wait_send)
    for copy in sent + [go_copy] + far_copies + cot_copies + wide_a[0] + wide_a[1] + wide_b[0] + wide_b[1] + att_copies + y_copies[0] + y_copies[1] + [c for hop in hops for c in hop]:
        copy.wait_send()


def local_part(query_key_value, cotangent, proj_weight, layer_scale, lengths):
    any_space = pl.BlockSpec(memory_space=pl.ANY)
    vmem = pl.BlockSpec(memory_space=pltpu.VMEM)
    grad, window = pl.pallas_call(
        kernel,
        out_shape=(
            jax.ShapeDtypeStruct((3, ROWS, HD), BF16),
            jax.ShapeDtypeStruct((200, SHARD), F32),
        ),
        in_specs=[any_space, any_space, any_space, any_space, pl.BlockSpec(memory_space=pltpu.SMEM)],
        out_specs=(any_space, vmem),
        scratch_shapes=[
            pltpu.VMEM((3, ROWS, HD), BF16),
            pltpu.VMEM((2, ROWS, D), BF16),
            pltpu.VMEM((1, D), F32),
            pltpu.VMEM((2, HD, ROWS), BF16),
            pltpu.VMEM((MAIN, MAIN), F32),
            pltpu.VMEM((TAIL, TAIL), F32),
            pltpu.VMEM((HEADS, MAIN, MAIN), F32),
            pltpu.VMEM((HEADS, TAIL, TAIL), F32),
            pltpu.VMEM((4, 4, SHARD, FIRST), BF16),
            pltpu.VMEM((4, 4, SHARD, LAST), BF16),
            pltpu.VMEM((HD, HALF), BF16),
            pltpu.VMEM((ROWS, HD), F32),
            pltpu.VMEM((ROWS, HD), BF16),
            pltpu.VMEM((ROWS, HD), BF16),
            pltpu.VMEM((4, 4, CHUNK, 384), BF16),
            pltpu.VMEM((4, 4, CHUNK, 256), BF16),
            pltpu.VMEM((4, 3, CHUNK, 384), BF16),
            pltpu.VMEM((4, 3, CHUNK, 256), BF16),
            pltpu.VMEM((4, CHUNK, 384), BF16),
            pltpu.VMEM((4, CHUNK, 256), BF16),
            pltpu.VMEM((3, CHUNK, 384), BF16),
            pltpu.VMEM((3, CHUNK, 256), BF16),
            pltpu.VMEM((2, SHARD, 384), BF16),
            pltpu.VMEM((2, SHARD, 256), BF16),
            pltpu.VMEM((7, SHARD, 384), BF16),
            pltpu.VMEM((SHARD, 512), F32),
            pltpu.VMEM((512, SHARD), F32),
            pltpu.VMEM((2, ROWS, SEAM), BF16),
            pltpu.VMEM((4, 2, SHARD, SEAM), BF16),
            pltpu.VMEM((4, 3, SHARD, SEAM), BF16),
            pltpu.VMEM((4, SHARD, SEAM), BF16),
            pltpu.VMEM((3, SHARD, SEAM), BF16),
            pltpu.VMEM((SHARD, SEAM), BF16),
            pltpu.VMEM((7, SHARD, 128), BF16),
            pltpu.SemaphoreType.DMA((N_MSG,)),
            pltpu.SemaphoreType.DMA((N_MSG,)),
            pltpu.SemaphoreType.DMA((18,)),
        ],
        compiler_params=pltpu.CompilerParams(
            collective_id=0, has_side_effects=True, vmem_limit_bytes=62 * 2**20
        ),
        name="attention_block",
    )(query_key_value, cotangent, proj_weight, layer_scale, lengths)
    return grad, window.T


def solution(mesh):
    placed = (
        P(None, ("dp", "fsdp"), None),
        P(("dp", "fsdp"), None),
        P("fsdp", None),
        P(),
        P(None, "fsdp", None),
    )
    return jax.shard_map(
        local_part,
        mesh=mesh,
        in_specs=placed,
        out_specs=(P(None, ("dp", "fsdp"), None), P("fsdp", "dp")),
        check_vma=False,
    )
```
